32 devices in a mesh: lat: 8 (over y, x, core), lon: 4 (over z).
Axes of the slice: x: 2, y: 2, z: 4, core: 2. Of those that a mesh axis runs over, the one named last changes fastest.
Arguments:
- grid_state: bfloat16 [120, 192, 128], P('lat', 'lon'), may hold values from -6 to 6
- weight_in: bfloat16 [6, 128, 384], replicated, may hold values from -0.5 to 0.5
- bias_in: float32 [6, 384], replicated, may hold values from -4 to 4
- weight_out: bfloat16 [6, 384, 128], replicated, may hold values from -0.3125 to 0.3125
- quad_weights: float32 [120], replicated, may hold values from 0.5 to 2
- diffusion: float32 [128], replicated, may hold values from 0.3 to 30
- legendre: bfloat16 [32, 120, 32], P('lon'), may hold values from -0.5 to 0.5
- chan_table: int32 [128], replicated, may hold values from 0 to 127, each once
- wave_table: int32 [32], replicated, may hold values from 0 to 31, each once
Outputs:
- updated: bfloat16 [120, 192, 128], P('lat', 'lon')
- spectral: float32 [32, 128, 2, 32], P('lon', 'lat')
The draws below stay inside these ranges and needn't reach their ends.
Inputs may be any that keep to these rules, and one draw needn't show every extreme that they name: `chan_table`: each channel 0 to 127 stands exactly once. `wave_table`: each wavenumber 0 to 31 stands exactly once.
All inputs are finite; a program needn't handle non-finite values.
Results may differ from the reference program's by a relative error of at most 0.012.
Values may be sent and summed in bfloat16 or wider, within the bound.
A program may use at most 64 MiB of HBM per device.

```python
import math
import jax
import jax.numpy as jnp
from jax import lax

H = 384
LAYERS = 6
C = 128
NLAT = 120
NLON = 192
MW = 32
NT = 32


def levels(key, dims, cuts, least, top_value):
    def one(dim, parts):
        steps = jax.random.uniform(jax.random.fold_in(jax.random.fold_in(key, 6), dim), (parts,), jnp.float32, least / len(cuts), top_value / len(cuts))
        return jnp.repeat(jnp.exp(steps), dims[dim] // parts).reshape((-1,) + (1,) * (len(dims) - dim - 1))

    level = one(*cuts[0])
    for cut in cuts[1:]:
        level = level * one(*cut)
    return level


def centred(rng, dims, deviation, limit, shards=(), kind=jnp.bfloat16):
    drawn = jax.random.normal(rng, dims, jnp.float32) * deviation
    if len(shards) > 0:
        drawn = levels(rng, dims, shards, -0.22, 0.18) * drawn
    return jnp.clip(drawn, min=-limit, max=limit).astype(kind)


def setup_inputs(seed: int = 0) -> dict:
    splits = jax.random.split(jax.random.key(seed), 10)
    return {
        "grid_state": centred(splits[0], (NLAT, NLON, C), 1.0, 6.0, ((0, 8), (1, 4))),
        "weight_in": centred(splits[1], (LAYERS, C, H), C ** -0.5, 0.5),
        "bias_in": centred(splits[2], (LAYERS, H), 1.0, 4.0, (), jnp.float32),
        "weight_out": centred(splits[3], (LAYERS, H, C), H ** -0.5, 0.3125),
        "quad_weights": jnp.clip(jnp.exp(jax.random.uniform(splits[4], (NLAT,), jnp.float32, math.log(0.5), math.log(2.0))), 0.5, 2.0),
        "diffusion": jnp.clip(jnp.exp(jax.random.uniform(splits[5], (C,), jnp.float32, math.log(0.3), math.log(30.0))), 0.3, 30.0),
        "legendre": centred(splits[6], (MW, NLAT, NT), NLAT ** -0.5, 0.5, ((0, 4),)),
        "chan_table": jax.random.permutation(splits[7], C).astype(jnp.int32),
        "wave_table": jax.random.permutation(splits[8], MW).astype(jnp.int32),
    }


def column_layers(column_rows, weight_in, bias_in, weight_out):
    hidden_state = column_rows.astype(jnp.float32)
    for layer_idx in range(weight_in.shape[0]):
        inv_rms = lax.rsqrt(lax.optimization_barrier(jnp.mean(hidden_state * hidden_state, axis=-1, keepdims=True)) + 1e-06)
        normed = (hidden_state * inv_rms).astype(jnp.bfloat16)
        pre_act = jnp.dot(normed, weight_in[layer_idx], preferred_element_type=jnp.float32) + bias_in[layer_idx]
        activation = jax.nn.gelu(pre_act, approximate=True).astype(jnp.bfloat16)
        hidden_state = hidden_state + jnp.dot(activation, weight_out[layer_idx], preferred_element_type=jnp.float32)
    return hidden_state.astype(jnp.bfloat16)

def trig_table(wave_ids, longitudes, lon_total):
    phase_angle = (wave_ids[:, None] * longitudes[None, :] % lon_total).astype(jnp.float32) * (2.0 * math.pi / lon_total)
    stacked = jnp.stack([jnp.cos(phase_angle), -jnp.sin(phase_angle)], axis=1) / math.sqrt(lon_total)
    return stacked.astype(jnp.bfloat16)

def reference(grid_state, weight_in, bias_in, weight_out, quad_weights, diffusion, legendre, chan_table, wave_table):
    columns = lax.map(lambda lat_row: column_layers(lat_row, weight_in, bias_in, weight_out), grid_state)
    ordered = jnp.take(columns, chan_table, axis=2)
    trig_rows = trig_table(wave_table, jnp.arange(NLON, dtype=jnp.int32), NLON)
    fourier = jnp.einsum('srj,ljk->skrl', trig_rows.astype(jnp.float32), ordered.astype(jnp.float32))
    weighted = (fourier * quad_weights).astype(jnp.bfloat16)
    raw_spec = jnp.einsum('skrl,sln->skrn', weighted.astype(jnp.float32), legendre.astype(jnp.float32))
    degree = jnp.arange(NT, dtype=jnp.int32)
    triangle = (degree[None, :] >= wave_table[:, None]).astype(jnp.float32)
    degree_f = degree.astype(jnp.float32)
    damping = jnp.take(diffusion, chan_table)[:, None] * (degree_f * (degree_f + 1.0))[None, :] / float(NT * NT)
    spectral = raw_spec * triangle[:, None, None, :] / (1.0 + damping)[None, :, None, :]
    spec_low = spectral.astype(jnp.bfloat16)
    back_fourier = jnp.einsum('skrn,sln->skrl', spec_low.astype(jnp.float32), legendre.astype(jnp.float32)).astype(jnp.bfloat16)
    tendency = jnp.einsum('skrl,srj->ljk', back_fourier.astype(jnp.float32), trig_rows.astype(jnp.float32)).astype(jnp.bfloat16)
    tendency = jnp.take(tendency, jnp.argsort(chan_table), axis=2)
    updated = (columns.astype(jnp.float32) + tendency.astype(jnp.float32)).astype(jnp.bfloat16)
    return (updated, spectral)
```

```python
import math

import jax
import jax.numpy as jnp
from jax import lax
from jax.sharding import PartitionSpec as P


def column_layers(column_rows, weight_in, bias_in, weight_out):
    hidden_state = column_rows.astype(jnp.float32)
    for layer_idx in range(weight_in.shape[0]):
        inv_rms = lax.rsqrt(jnp.mean(hidden_state * hidden_state, axis=-1, keepdims=True) + 1e-06)
        normed = (hidden_state * inv_rms).astype(jnp.bfloat16)
        pre_act = (
            jnp.dot(normed, weight_in[layer_idx], preferred_element_type=jnp.float32)
            + bias_in[layer_idx]
        )
        activation = jax.nn.gelu(pre_act, approximate=True).astype(jnp.bfloat16)
        hidden_state = hidden_state + jnp.dot(
            activation, weight_out[layer_idx], preferred_element_type=jnp.float32
        )
    return hidden_state.astype(jnp.bfloat16)


def trig_table(wave_ids, longitudes, lon_total):
    phase_angle = (wave_ids[:, None] * longitudes[None, :] % lon_total).astype(jnp.float32) * (
        2.0 * math.pi / lon_total
    )
    stacked = jnp.stack([jnp.cos(phase_angle), -jnp.sin(phase_angle)], axis=1) / math.sqrt(
        lon_total
    )
    return stacked.astype(jnp.bfloat16)


def pick_channels(rows, chosen):
    picked = jnp.einsum("ljc,ck->ljk", rows, chosen, preferred_element_type=jnp.float32)
    return picked.astype(jnp.bfloat16)


def local(
    grid_state,
    weight_in,
    bias_in,
    weight_out,
    quad_weights,
    diffusion,
    legendre,
    chan_table,
    wave_table,
):
    lat_rows, lon_cols, channels = grid_state.shape
    lat_count = lax.axis_size("lat")
    lon_count = lax.axis_size("lon")
    lon_total = lon_cols * lon_count
    per_dev = channels // lat_count
    owned_slots = legendre.shape[0]
    top_degree = legendre.shape[2]
    flat_rows = grid_state.reshape(lat_rows * lon_cols, channels)
    columns = column_layers(flat_rows, weight_in, bias_in, weight_out).reshape(
        lat_rows, lon_cols, channels
    )
    every = jnp.arange(channels, dtype=jnp.int32)
    chosen = (every[:, None] == chan_table[None, :]).astype(jnp.bfloat16)
    ordered = pick_channels(columns, chosen)
    levels = lax.all_to_all(ordered, "lat", split_axis=2, concat_axis=0, tiled=True)
    trig_all = trig_table(wave_table, jnp.arange(lon_total, dtype=jnp.int32), lon_total)
    lon_here = lax.axis_index("lon") * lon_cols + jnp.arange(lon_cols, dtype=jnp.int32)
    trig_rows = trig_table(wave_table, lon_here, lon_total)
    fourier = lax.psum_scatter(
        jnp.einsum("srj,ljk->skrl", trig_rows, levels, preferred_element_type=jnp.float32),
        "lon",
        scatter_dimension=0,
        tiled=True,
    )
    weighted = (fourier * quad_weights).astype(jnp.bfloat16)
    raw_spec = jnp.einsum("skrl,sln->skrn", weighted, legendre, preferred_element_type=jnp.float32)
    my_waves = lax.dynamic_slice_in_dim(
        wave_table, lax.axis_index("lon") * owned_slots, owned_slots, 0
    )
    degree = jnp.arange(top_degree, dtype=jnp.int32)
    triangle = (degree[None, :] >= my_waves[:, None]).astype(jnp.float32)
    my_chans = lax.dynamic_slice_in_dim(chan_table, lax.axis_index("lat") * per_dev, per_dev, 0)
    degree_f = degree.astype(jnp.float32)
    damping = (
        jnp.sum(jnp.where(my_chans[:, None] == every[None, :], diffusion[None, :], 0.0), 1)[:, None]
        * (degree_f * (degree_f + 1.0))[None, :]
        / float(top_degree * top_degree)
    )
    spectral = raw_spec * triangle[:, None, None, :] / (1.0 + damping)[None, :, None, :]
    back_fourier = jnp.einsum(
        "skrn,sln->skrl",
        spectral.astype(jnp.bfloat16),
        legendre,
        preferred_element_type=jnp.float32,
    ).astype(jnp.bfloat16)
    all_waves = lax.all_to_all(back_fourier, "lon", split_axis=3, concat_axis=0, tiled=True)
    band_tendency = jnp.einsum(
        "skrl,srj->ljk", all_waves, trig_all, preferred_element_type=jnp.float32
    ).astype(jnp.bfloat16)
    tendency = lax.all_to_all(
        lax.all_to_all(band_tendency, "lon", split_axis=1, concat_axis=0, tiled=True),
        "lat",
        split_axis=0,
        concat_axis=2,
        tiled=True,
    )
    tendency = pick_channels(tendency, chosen.T)
    updated = (columns.astype(jnp.float32) + tendency.astype(jnp.float32)).astype(jnp.bfloat16)
    return (updated, spectral)


def solution(mesh):
    placed = (P("lat", "lon", None), P(), P(), P(), P(), P(), P("lon", None, None), P(), P())
    return jax.shard_map(
        local,
        mesh=mesh,
        in_specs=placed,
        out_specs=(P("lat", "lon", None), P("lon", "lat", None, None)),
        check_vma=False,
    )
```

```python
import functools
import math

import jax
import jax.numpy as jnp
from jax import lax
from jax.experimental import pallas as pl
from jax.experimental.pallas import tpu as pltpu
from jax.sharding import PartitionSpec as P

MESH = pl.DeviceIdType.MESH
PART = 3
GELU_A = math.sqrt(2.0 / math.pi)
GELU_B = 0.044715 * GELU_A


def column_layers(column_rows, weight_in, bias_in, weight_out):
    hidden_state = column_rows.astype(jnp.float32)
    for layer_idx in range(weight_in.shape[0]):
        inv_rms = lax.rsqrt(jnp.mean(hidden_state * hidden_state, axis=-1, keepdims=True) + 1e-06)
        normed = (hidden_state * inv_rms).astype(jnp.bfloat16)
        pre_act = (
            jnp.dot(normed, weight_in[layer_idx], preferred_element_type=jnp.float32)
            + bias_in[layer_idx]
        )
        activation = jax.nn.gelu(pre_act, approximate=True).astype(jnp.bfloat16)
        hidden_state = hidden_state + jnp.dot(
            activation, weight_out[layer_idx], preferred_element_type=jnp.float32
        )
    return hidden_state.astype(jnp.bfloat16)


def trig_table(wave_ids, longitudes, lon_total):
    phase_angle = (wave_ids[:, None] * longitudes[None, :] % lon_total).astype(jnp.float32) * (
        2.0 * math.pi / lon_total
    )
    stacked = jnp.stack([jnp.cos(phase_angle), -jnp.sin(phase_angle)], axis=1) / math.sqrt(
        lon_total
    )
    return stacked.astype(jnp.bfloat16)


def pick_channels(rows, chosen):
    picked = jnp.einsum("ljc,ck->ljk", rows, chosen, preferred_element_type=jnp.float32)
    return picked.astype(jnp.bfloat16)


def local(
    grid_state,
    weight_in,
    bias_in,
    weight_out,
    quad_weights,
    diffusion,
    legendre,
    chan_table,
    wave_table,
):
    lat_rows, lon_cols, channels = grid_state.shape
    lat_count = lax.axis_size("lat")
    lon_count = lax.axis_size("lon")
    lon_total = lon_cols * lon_count
    per_dev = channels // lat_count
    owned_slots = legendre.shape[0]
    top_degree = legendre.shape[2]
    flat_rows = grid_state.reshape(lat_rows * lon_cols, channels)
    columns = column_layers(flat_rows, weight_in, bias_in, weight_out).reshape(
        lat_rows, lon_cols, channels
    )
    every = jnp.arange(channels, dtype=jnp.int32)
    chosen = (every[:, None] == chan_table[None, :]).astype(jnp.bfloat16)
    ordered = pick_channels(columns, chosen)
    levels = lax.all_to_all(ordered, "lat", split_axis=2, concat_axis=0, tiled=True)
    trig_all = trig_table(wave_table, jnp.arange(lon_total, dtype=jnp.int32), lon_total)
    lon_here = lax.axis_index("lon") * lon_cols + jnp.arange(lon_cols, dtype=jnp.int32)
    trig_rows = trig_table(wave_table, lon_here, lon_total)
    fourier = lax.psum_scatter(
        jnp.einsum("srj,ljk->skrl", trig_rows, levels, preferred_element_type=jnp.float32),
        "lon",
        scatter_dimension=0,
        tiled=True,
    )
    weighted = (fourier * quad_weights).astype(jnp.bfloat16)
    raw_spec = jnp.einsum("skrl,sln->skrn", weighted, legendre, preferred_element_type=jnp.float32)
    my_waves = lax.dynamic_slice_in_dim(
        wave_table, lax.axis_index("lon") * owned_slots, owned_slots, 0
    )
    degree = jnp.arange(top_degree, dtype=jnp.int32)
    triangle = (degree[None, :] >= my_waves[:, None]).astype(jnp.float32)
    my_chans = lax.dynamic_slice_in_dim(chan_table, lax.axis_index("lat") * per_dev, per_dev, 0)
    degree_f = degree.astype(jnp.float32)
    damping = (
        jnp.sum(jnp.where(my_chans[:, None] == every[None, :], diffusion[None, :], 0.0), 1)[:, None]
        * (degree_f * (degree_f + 1.0))[None, :]
        / float(top_degree * top_degree)
    )
    spectral = raw_spec * triangle[:, None, None, :] / (1.0 + damping)[None, :, None, :]
    back_fourier = jnp.einsum(
        "skrn,sln->skrl",
        spectral.astype(jnp.bfloat16),
        legendre,
        preferred_element_type=jnp.float32,
    ).astype(jnp.bfloat16)
    all_waves = lax.all_to_all(back_fourier, "lon", split_axis=3, concat_axis=0, tiled=True)
    band_tendency = jnp.einsum(
        "skrl,srj->ljk", all_waves, trig_all, preferred_element_type=jnp.float32
    ).astype(jnp.bfloat16)
    tendency = lax.all_to_all(
        lax.all_to_all(band_tendency, "lon", split_axis=1, concat_axis=0, tiled=True),
        "lat",
        split_axis=0,
        concat_axis=2,
        tiled=True,
    )
    tendency = pick_channels(tendency, chosen.T)
    updated = (columns.astype(jnp.float32) + tendency.astype(jnp.float32)).astype(jnp.bfloat16)
    return (updated, spectral)

def spread(blocks, width):
    blocks = list(blocks)
    group = lax.broadcasted_iota(jnp.int32, blocks[0].shape, 1) // width
    lanes = blocks[0].shape[1]
    step = 1
    while step < len(blocks):
        upper = (group & step) != 0
        for i in range(len(blocks)):
            if i & step == 0:
                low, high = blocks[i], blocks[i + step]
                blocks[i] = jnp.where(upper, pltpu.roll(high, step * width, 1), low)
                blocks[i + step] = jnp.where(
                    upper, high, pltpu.roll(low, lanes - step * width, 1)
                )
        step *= 2
    return blocks


def fused_kernel(
    lat_count,
    lon_count,
    lat_rows,
    lon_cols,
    grid_ref,
    w_in_ref,
    bias_ref,
    w_out_ref,
    quad_ref,
    diff_ref,
    leg_ref,
    chan_ref,
    wave_ref,
    out_ref,
    spec_ref,
    cols_ref,
    rows_ref,
    send1,
    recv1,
    send2,
    recv2,
    send_sem1,
    recv_sem1,
    send_sem2,
    recv_sem2,
):
    f32, bf16, i32 = jnp.float32, jnp.bfloat16, jnp.int32
    iota = lambda shape, dim: lax.broadcasted_iota(i32, shape, dim)
    channels = grid_ref.shape[1]
    layers = w_in_ref.shape[0]
    slots, lat_total, top = leg_ref.shape
    waves = wave_ref.shape[1]
    per_dev = channels // lat_count
    devices = lat_count * lon_count
    pad = send1.shape[1]
    wide = send1.shape[2]
    trig_rows = 2 * waves
    lon_total = lon_cols * lon_count
    my_lat, my_lon = lax.axis_index("lat"), lax.axis_index("lon")
    me = my_lat * lon_count + my_lon

    barrier = pltpu.get_barrier_semaphore()

    def peer(i):
        other = lax.rem(me + i, devices)
        return other, {"lat": other // lon_count, "lon": lax.rem(other, lon_count)}

    @pl.loop(1, devices)
    def _(i):
        pl.semaphore_signal(barrier, inc=1, device_id=peer(i)[1], device_id_type=MESH)

    def column_of(row, size):
        eye = iota((size, size), 0) == iota((size, size), 1)
        return jnp.sum(jnp.where(eye, row, jnp.zeros_like(row)), 1, keepdims=True)

    chan_row = chan_ref[...]
    chosen = iota((channels, channels), 0) == chan_row
    order = jnp.where(chosen, 1.0, 0.0).astype(bf16)
    unorder = jnp.where(iota((channels, channels), 1) == column_of(chan_row, channels), 1.0, 0.0)
    unorder = unorder.astype(bf16)

    wave_f = wave_ref[...].astype(f32)
    wave_col = column_of(wave_f, waves)

    def slot_of(row):
        inner = row & (2 * slots - 1)
        return (row // (2 * slots)) * slots + (inner & (slots - 1)), inner // slots

    def trig(wave, part, place):
        angle = wave * place
        angle = angle + part * (lon_total / 4.0)
        angle = angle - lon_total * jnp.floor((angle + 0.5) * (1.0 / lon_total))
        return jnp.cos(angle * (2.0 * math.pi / lon_total)) * (1.0 / math.sqrt(lon_total))

    slot_a, part_a = slot_of(iota((trig_rows, 1), 0))
    wave_a = jnp.sum(jnp.where(iota((trig_rows, waves), 1) == slot_a, wave_f, 0.0), 1, keepdims=True)
    lon_a = (iota((trig_rows, lon_cols), 1) + my_lon * lon_cols).astype(f32)
    trig_in = trig(wave_a, part_a.astype(f32), lon_a).astype(bf16)
    slot_b, part_b = slot_of(iota((1, trig_rows), 1))
    wave_b = jnp.sum(jnp.where(iota((waves, trig_rows), 0) == slot_b, wave_col, 0.0), 0, keepdims=True)
    lon_b = (iota((lon_cols, trig_rows), 0) + my_lon * lon_cols).astype(f32)
    trig_out = trig(wave_b, part_b.astype(f32), lon_b).astype(bf16)

    rows_ref[...] = jnp.zeros_like(rows_ref)

    part_rows = PART * lon_cols

    def column_part(p, carry):
        start = pl.multiple_of(p * part_rows, part_rows)
        x = grid_ref[pl.ds(start, part_rows), :].astype(f32)
        for layer in range(layers):
            inv = lax.rsqrt(jnp.mean(x * x, axis=-1, keepdims=True) + 1e-06)
            normed = (x * inv).astype(bf16)
            pre = jnp.dot(normed, w_in_ref[layer], preferred_element_type=f32)
            pre = pre + bias_ref[pl.ds(layer, 1), :]
            inner = pre * (GELU_A + GELU_B * (pre * pre))
            half = 0.5 * pre
            act = (half + half * jnp.tanh(inner)).astype(bf16)
            x = x + jnp.dot(act, w_out_ref[layer], preferred_element_type=f32)
        cols = x.astype(bf16)
        cols_ref[pl.ds(start, part_rows), :] = cols
        ordered = jnp.dot(cols, order, preferred_element_type=f32).astype(bf16)
        for q in range(PART):
            partial = jnp.dot(
                trig_in, ordered[q * lon_cols : (q + 1) * lon_cols], preferred_element_type=f32
            )
            rows_ref[pl.ds(p * PART + q, trig_rows, stride=pad), :] = partial
        return carry

    lax.fori_loop(0, lat_rows // PART, column_part, 0)

    for b in range(lon_count):
        for r in range(2):
            first = (b * 2 + r) * slots
            got = spread(
                [rows_ref[(first + s) * pad : (first + s + 1) * pad, :] for s in range(slots)], per_dev
            )
            for a in range(lat_count):
                send1[a * lon_count + b, :, r * channels : (r + 1) * channels] = got[a].astype(bf16)

    pl.semaphore_wait(barrier, devices - 1)

    def exchange(send, recv, send_sem, recv_sem, chunk_of):
        def copy(i):
            other, place = peer(i)
            return pltpu.make_async_remote_copy(
                src_ref=send.at[chunk_of(other)],
                dst_ref=recv.at[me],
                send_sem=send_sem.at[other],
                recv_sem=recv_sem.at[me],
                device_id=place,
                device_id_type=MESH,
            )

        @pl.loop(1, devices)
        def _(i):
            copy(i).start()

        recv[me] = send[chunk_of(me)]

        def finish():
            @pl.loop(1, devices)
            def _(i):
                other, place = peer(i)
                pltpu.make_async_remote_copy(
                    src_ref=send.at[chunk_of(other)],
                    dst_ref=recv.at[other],
                    send_sem=send_sem.at[other],
                    recv_sem=recv_sem.at[other],
                    device_id=place,
                    device_id_type=MESH,
                ).wait()

        return finish

    finish = exchange(send1, recv1, send_sem1, recv_sem1, lambda other: other)

    lat_pad = lat_count * pad
    spect = slots * top
    inner_row = iota((lat_pad, lat_total), 0)
    lat_of = jnp.where(
        (inner_row & (pad - 1)) < lat_rows, (inner_row // pad) * lat_rows + (inner_row & (pad - 1)), -1
    )
    chosen_lat = lat_of == iota((lat_pad, lat_total), 1)
    quad_col = jnp.sum(jnp.where(chosen_lat, quad_ref[...], 0.0), 1, keepdims=True)
    place_lat = jnp.where(chosen_lat, 1.0, 0.0).astype(bf16)
    leg = jnp.zeros((lat_pad, spect), f32)
    for s in range(slots):
        rows = jnp.dot(place_lat, leg_ref[s], preferred_element_type=f32).astype(bf16)
        into = iota((top, spect), 1) == iota((top, spect), 0) + s * top
        leg = leg + jnp.dot(rows, jnp.where(into, 1.0, 0.0).astype(bf16), preferred_element_type=f32)
    leg_t = jnp.transpose(leg).astype(bf16)
    leg = leg.astype(bf16)

    diff_col = column_of(diff_ref[...], channels)
    diff_row = jnp.sum(jnp.where(chosen, diff_col, 0.0), 0, keepdims=True)
    diff_sorted = column_of(diff_row, channels)
    lane = iota((channels, wide), 1)
    mine = iota((channels, wide), 0) == (lane & (per_dev - 1)) + my_lat * per_dev
    diff_lane = jnp.sum(jnp.where(mine, diff_sorted, 0.0), 0, keepdims=True)
    row_n = iota((spect, 1), 0)
    degree = (row_n & (top - 1)).astype(f32)
    damping = diff_lane * (degree * (degree + 1.0)) / float(top * top)
    slot_n = row_n // top
    wave_n = jnp.sum(
        jnp.where(iota((spect, waves), 1) == slot_n + my_lon * slots, wave_f, 0.0), 1, keepdims=True
    )
    lane_slot = (iota((spect, wide), 1) & (channels - 1)) // per_dev
    kept = (lane_slot == slot_n) & (degree >= wave_n)
    scale = 1.0 / (1.0 + damping)

    finish()
    fourier = jnp.zeros((lat_pad, wide), f32)
    for b in range(lon_count):
        for_lon = jnp.concatenate([recv1[a * lon_count + b] for a in range(lat_count)], 0)
        fourier = fourier + for_lon.astype(f32)
    weighted = (fourier * quad_col).astype(bf16)
    raw = jnp.dot(leg_t, weighted, preferred_element_type=f32)
    spectral = jnp.where(kept, raw * scale, 0.0)
    back = jnp.dot(leg, spectral.astype(bf16), preferred_element_type=f32).astype(bf16)
    for a in range(lat_count):
        send2[a] = back[a * pad : (a + 1) * pad]
    finish = exchange(send2, recv2, send_sem2, recv_sem2, lambda other: other // lon_count)
    folded = spectral[:top]
    for s in range(1, slots):
        folded = folded + spectral[s * top : (s + 1) * top]
    spec_ref[...] = folded
    finish()

    for b in range(lon_count):
        for r in range(2):
            first = (b * 2 + r) * slots
            got = spread(
                [
                    recv2[a * lon_count + b, :, r * channels : (r + 1) * channels].astype(f32)
                    for a in range(lat_count)
                ],
                per_dev,
            )
            whole = jnp.concatenate(got, 0).astype(bf16)
            rows_ref[first * pad : (first + slots) * pad, :] = jnp.dot(
                whole, unorder, preferred_element_type=f32
            )
    for l in range(lat_rows):
        coeffs = rows_ref[pl.ds(l, trig_rows, stride=pad), :].astype(bf16)
        tendency = jnp.dot(trig_out, coeffs, preferred_element_type=f32).astype(bf16)
        here = slice(l * lon_cols, (l + 1) * lon_cols)
        out_ref[here, :] = (cols_ref[here, :].astype(f32) + tendency.astype(f32)).astype(bf16)


def fused(
    grid_state,
    weight_in,
    bias_in,
    weight_out,
    quad_weights,
    diffusion,
    legendre,
    chan_table,
    wave_table,
):
    lat_rows, lon_cols, channels = grid_state.shape
    lat_count = lax.axis_size("lat")
    lon_count = lax.axis_size("lon")
    slots, _, top = legendre.shape
    waves = wave_table.shape[0]
    devices = lat_count * lon_count
    pad = 16
    wide = 2 * channels
    vmem = pl.BlockSpec(memory_space=pltpu.VMEM)
    updated, spec = pl.pallas_call(
        functools.partial(fused_kernel, lat_count, lon_count, lat_rows, lon_cols),
        out_shape=(
            jax.ShapeDtypeStruct((lat_rows * lon_cols, channels), jnp.bfloat16),
            jax.ShapeDtypeStruct((top, wide), jnp.float32),
        ),
        in_specs=[vmem] * 9,
        out_specs=(vmem, vmem),
        scratch_shapes=[
            pltpu.VMEM((lat_rows * lon_cols, channels), jnp.bfloat16),
            pltpu.VMEM((2 * waves * pad, channels), jnp.float32),
            pltpu.VMEM((devices, pad, wide), jnp.bfloat16),
            pltpu.VMEM((devices, pad, wide), jnp.bfloat16),
            pltpu.VMEM((lat_count, pad, wide), jnp.bfloat16),
            pltpu.VMEM((devices, pad, wide), jnp.bfloat16),
            pltpu.SemaphoreType.DMA((devices,)),
            pltpu.SemaphoreType.DMA((devices,)),
            pltpu.SemaphoreType.DMA((devices,)),
            pltpu.SemaphoreType.DMA((devices,)),
        ],
        compiler_params=pltpu.CompilerParams(
            collective_id=0, has_side_effects=True, vmem_limit_bytes=40 * 2**20
        ),
    )(
        grid_state.reshape(lat_rows * lon_cols, channels),
        weight_in,
        bias_in,
        weight_out,
        quad_weights[None, :],
        diffusion[None, :],
        legendre,
        chan_table[None, :],
        wave_table[None, :],
    )
    spectral = spec.reshape(top, 2, slots, channels // lat_count).transpose(2, 3, 1, 0)
    return updated.reshape(lat_rows, lon_cols, channels), spectral


def by_size(*arrays):
    grid_state, legendre, wave_table = arrays[0], arrays[6], arrays[8]
    lat_rows, lon_cols, channels = grid_state.shape
    slots, _, top = legendre.shape
    fits = (
        channels == 128
        and slots == lax.axis_size("lat")
        and slots & (slots - 1) == 0
        and top & (top - 1) == 0
        and slots * lax.axis_size("lon") == wave_table.shape[0]
        and lat_rows <= 16
        and lat_rows % PART == 0
        and lon_cols % 16 == 0
    )
    return (fused if fits else local)(*arrays)


def solution(mesh):
    placed = (P("lat", "lon", None), P(), P(), P(), P(), P(), P("lon", None, None), P(), P())
    return jax.shard_map(
        by_size,
        mesh=mesh,
        in_specs=placed,
        out_specs=(P("lat", "lon", None), P("lon", "lat", None, None)),
        check_vma=False,
    )
```

```python
import functools
import math

import jax
import jax.numpy as jnp
from jax import lax
from jax.experimental import pallas as pl
from jax.experimental.pallas import tpu as pltpu
from jax.sharding import PartitionSpec as P

MESH = pl.DeviceIdType.MESH
WEIGHTS = pl.ANY
GELU_A = math.sqrt(2.0 / math.pi)
GELU_B = 0.044715 * GELU_A


def column_layers(column_rows, weight_in, bias_in, weight_out):
    hidden_state = column_rows.astype(jnp.float32)
    for layer_idx in range(weight_in.shape[0]):
        inv_rms = lax.rsqrt(jnp.mean(hidden_state * hidden_state, axis=-1, keepdims=True) + 1e-06)
        normed = (hidden_state * inv_rms).astype(jnp.bfloat16)
        pre_act = (
            jnp.dot(normed, weight_in[layer_idx], preferred_element_type=jnp.float32)
            + bias_in[layer_idx]
        )
        activation = jax.nn.gelu(pre_act, approximate=True).astype(jnp.bfloat16)
        hidden_state = hidden_state + jnp.dot(
            activation, weight_out[layer_idx], preferred_element_type=jnp.float32
        )
    return hidden_state.astype(jnp.bfloat16)


def trig_table(wave_ids, longitudes, lon_total):
    phase_angle = (wave_ids[:, None] * longitudes[None, :] % lon_total).astype(jnp.float32) * (
        2.0 * math.pi / lon_total
    )
    stacked = jnp.stack([jnp.cos(phase_angle), -jnp.sin(phase_angle)], axis=1) / math.sqrt(
        lon_total
    )
    return stacked.astype(jnp.bfloat16)


def pick_channels(rows, chosen):
    picked = jnp.einsum("ljc,ck->ljk", rows, chosen, preferred_element_type=jnp.float32)
    return picked.astype(jnp.bfloat16)


def local(
    grid_state,
    weight_in,
    bias_in,
    weight_out,
    quad_weights,
    diffusion,
    legendre,
    chan_table,
    wave_table,
):
    lat_rows, lon_cols, channels = grid_state.shape
    lat_count = lax.axis_size("lat")
    lon_count = lax.axis_size("lon")
    lon_total = lon_cols * lon_count
    per_dev = channels // lat_count
    owned_slots = legendre.shape[0]
    top_degree = legendre.shape[2]
    flat_rows = grid_state.reshape(lat_rows * lon_cols, channels)
    columns = column_layers(flat_rows, weight_in, bias_in, weight_out).reshape(
        lat_rows, lon_cols, channels
    )
    every = jnp.arange(channels, dtype=jnp.int32)
    chosen = (every[:, None] == chan_table[None, :]).astype(jnp.bfloat16)
    ordered = pick_channels(columns, chosen)
    levels = lax.all_to_all(ordered, "lat", split_axis=2, concat_axis=0, tiled=True)
    trig_all = trig_table(wave_table, jnp.arange(lon_total, dtype=jnp.int32), lon_total)
    lon_here = lax.axis_index("lon") * lon_cols + jnp.arange(lon_cols, dtype=jnp.int32)
    trig_rows = trig_table(wave_table, lon_here, lon_total)
    fourier = lax.psum_scatter(
        jnp.einsum("srj,ljk->skrl", trig_rows, levels, preferred_element_type=jnp.float32),
        "lon",
        scatter_dimension=0,
        tiled=True,
    )
    weighted = (fourier * quad_weights).astype(jnp.bfloat16)
    raw_spec = jnp.einsum("skrl,sln->skrn", weighted, legendre, preferred_element_type=jnp.float32)
    my_waves = lax.dynamic_slice_in_dim(
        wave_table, lax.axis_index("lon") * owned_slots, owned_slots, 0
    )
    degree = jnp.arange(top_degree, dtype=jnp.int32)
    triangle = (degree[None, :] >= my_waves[:, None]).astype(jnp.float32)
    my_chans = lax.dynamic_slice_in_dim(chan_table, lax.axis_index("lat") * per_dev, per_dev, 0)
    degree_f = degree.astype(jnp.float32)
    damping = (
        jnp.sum(jnp.where(my_chans[:, None] == every[None, :], diffusion[None, :], 0.0), 1)[:, None]
        * (degree_f * (degree_f + 1.0))[None, :]
        / float(top_degree * top_degree)
    )
    spectral = raw_spec * triangle[:, None, None, :] / (1.0 + damping)[None, :, None, :]
    back_fourier = jnp.einsum(
        "skrn,sln->skrl",
        spectral.astype(jnp.bfloat16),
        legendre,
        preferred_element_type=jnp.float32,
    ).astype(jnp.bfloat16)
    all_waves = lax.all_to_all(back_fourier, "lon", split_axis=3, concat_axis=0, tiled=True)
    band_tendency = jnp.einsum(
        "skrl,srj->ljk", all_waves, trig_all, preferred_element_type=jnp.float32
    ).astype(jnp.bfloat16)
    tendency = lax.all_to_all(
        lax.all_to_all(band_tendency, "lon", split_axis=1, concat_axis=0, tiled=True),
        "lat",
        split_axis=0,
        concat_axis=2,
        tiled=True,
    )
    tendency = pick_channels(tendency, chosen.T)
    updated = (columns.astype(jnp.float32) + tendency.astype(jnp.float32)).astype(jnp.bfloat16)
    return (updated, spectral)

def spread(blocks, width):
    blocks = list(blocks)
    group = lax.broadcasted_iota(jnp.int32, blocks[0].shape, 1) // width
    lanes = blocks[0].shape[1]
    step = 1
    while step < len(blocks):
        upper = (group & step) != 0
        for i in range(len(blocks)):
            if i & step == 0:
                low, high = blocks[i], blocks[i + step]
                blocks[i] = jnp.where(upper, pltpu.roll(high, step * width, 1), low)
                blocks[i + step] = jnp.where(
                    upper, high, pltpu.roll(low, lanes - step * width, 1)
                )
        step *= 2
    return blocks


def fused_kernel(
    lat_count,
    lon_count,
    lat_rows,
    lon_cols,
    slots,
    grid_ref,
    w_in_hbm,
    bias_ref,
    w_out_hbm,
    quad_ref,
    diff_ref,
    leg_ref,
    chan_ref,
    wave_ref,
    out_ref,
    spec_ref,
    w_in_ref,
    w_out_ref,
    cols_ref,
    rows_ref,
    legs,
    send1,
    recv1,
    send2,
    recv2,
    low_ref,
    recv3,
    send4,
    recv4,
    w_sem,
    leg_send,
    leg_recv,
    lat_send1,
    lat_recv1,
    lon_send2,
    lon_recv2,
    lon_send3,
    lon_recv3,
    lat_send4,
    lat_recv4,
):
    f32, bf16, i32 = jnp.float32, jnp.bfloat16, jnp.int32
    iota = lambda shape, dim: lax.broadcasted_iota(i32, shape, dim)
    channels = grid_ref.shape[1]
    layers = w_in_ref.shape[0]
    spect, lat_total = leg_ref.shape
    top = spect // slots
    waves = wave_ref.shape[1]
    per_dev = channels // lat_count
    wide = 2 * channels
    trig_rows = 2 * waves
    lon_total = lon_cols * lon_count
    my_lat, my_lon = lax.axis_index("lat"), lax.axis_index("lon")

    loads = []
    for layer in range(layers):
        into = pltpu.make_async_copy(w_in_hbm.at[layer], w_in_ref.at[layer], w_sem.at[0, layer])
        out_of = pltpu.make_async_copy(w_out_hbm.at[layer], w_out_ref.at[layer], w_sem.at[1, layer])
        into.start()
        out_of.start()
        loads.append((into, out_of))

    barrier = pltpu.get_barrier_semaphore()

    def lat_peer(i):
        other = lax.rem(my_lat + i, lat_count)
        return other, {"lat": other, "lon": my_lon}

    def lon_peer(i):
        other = lax.rem(my_lon + i, lon_count)
        return other, {"lat": my_lat, "lon": other}

    for i in range(1, lat_count):
        pl.semaphore_signal(barrier, inc=1, device_id=lat_peer(i)[1], device_id_type=MESH)
    for i in range(1, lon_count):
        pl.semaphore_signal(barrier, inc=1, device_id=lon_peer(i)[1], device_id_type=MESH)

    def exchange(peer_of, count, mine, source, target, send_sem, recv_sem):
        waits = []
        for i in range(1, count):
            other, place = peer_of(i)
            pltpu.make_async_remote_copy(
                src_ref=source(other),
                dst_ref=target(mine),
                send_sem=send_sem(other),
                recv_sem=recv_sem(mine),
                device_id=place,
                device_id_type=MESH,
            ).start()
            waits.append(
                pltpu.make_async_remote_copy(
                    src_ref=source(other),
                    dst_ref=target(other),
                    send_sem=send_sem(other),
                    recv_sem=recv_sem(other),
                    device_id=place,
                    device_id_type=MESH,
                )
            )

        def finish():
            for w in waits:
                w.wait()

        return finish

    def column_of(row, size):
        eye = iota((size, size), 0) == iota((size, size), 1)
        return jnp.sum(jnp.where(eye, row, jnp.zeros_like(row)), 1, keepdims=True)

    chan_row = chan_ref[...]
    chosen = iota((channels, channels), 0) == chan_row
    order = jnp.where(chosen, 1.0, 0.0).astype(bf16)
    unorder = jnp.where(iota((channels, channels), 1) == column_of(chan_row, channels), 1.0, 0.0)
    unorder = unorder.astype(bf16)

    wave_f = wave_ref[...].astype(f32)
    wave_col = column_of(wave_f, waves)

    def slot_of(row):
        inner = row & (2 * slots - 1)
        return (row // (2 * slots)) * slots + (inner & (slots - 1)), inner // slots

    def trig(wave, part, place):
        angle = wave * place
        angle = angle + part * (lon_total / 4.0)
        angle = angle - lon_total * jnp.floor((angle + 0.5) * (1.0 / lon_total))
        return jnp.cos(angle * (2.0 * math.pi / lon_total)) * (1.0 / math.sqrt(lon_total))

    slot_a, part_a = slot_of(iota((trig_rows, 1), 0))
    wave_a = jnp.sum(jnp.where(iota((trig_rows, waves), 1) == slot_a, wave_f, 0.0), 1, keepdims=True)
    lon_a = (iota((trig_rows, lon_cols), 1) + my_lon * lon_cols).astype(f32)
    trig_in = trig(wave_a, part_a.astype(f32), lon_a).astype(bf16)
    slot_b, part_b = slot_of(iota((1, trig_rows), 1))
    wave_b = jnp.sum(jnp.where(iota((waves, trig_rows), 0) == slot_b, wave_col, 0.0), 0, keepdims=True)
    lon_b = (iota((lon_cols, trig_rows), 0) + my_lon * lon_cols).astype(f32)
    trig_out = trig(wave_b, part_b.astype(f32), lon_b).astype(bf16)

    lat_pad = 16 * lat_count

    def lat_of(place):
        row = (place // (8 * lat_count)) * 8 + (place & 7)
        device = (place // 8) & (lat_count - 1)
        return jnp.where(row < lat_rows, device * lat_rows + row, -1)

    by_row = lat_of(iota((lat_pad, lat_total), 0)) == iota((lat_pad, lat_total), 1)
    quad_col = jnp.sum(jnp.where(by_row, quad_ref[...], 0.0), 1, keepdims=True)
    lat_col = iota((lat_total, lat_pad), 0)
    by_col = jnp.where(lat_of(iota((lat_total, lat_pad), 1)) == lat_col, 1.0, 0.0).astype(bf16)
    legs[my_lon] = jnp.dot(leg_ref[...], by_col, preferred_element_type=f32).astype(bf16)

    def column_part(low, high, first):
        part = slice(low * lon_cols, high * lon_cols)
        x = grid_ref[part, :].astype(f32)
        for layer in range(layers):
            inv = lax.rsqrt(jnp.mean(x * x, axis=-1, keepdims=True) + 1e-06)
            normed = (x * inv).astype(bf16)
            if first:
                loads[layer][0].wait()
            pre = jnp.dot(normed, w_in_ref[layer], preferred_element_type=f32)
            pre = pre + bias_ref[pl.ds(layer, 1), :]
            inner = pre * (GELU_A + GELU_B * (pre * pre))
            half = 0.5 * pre
            act = (half + half * jnp.tanh(inner)).astype(bf16)
            if first:
                loads[layer][1].wait()
            x = x + jnp.dot(act, w_out_ref[layer], preferred_element_type=f32)
        cols = x.astype(bf16)
        cols_ref[part, :] = cols
        return jnp.dot(cols, order, preferred_element_type=f32).astype(bf16)

    def pack(h, low, high, ordered):
        for l in range(low, low + 8):
            if l < high:
                q = (l - low) * lon_cols
                partial = jnp.dot(trig_in, ordered[q : q + lon_cols], preferred_element_type=f32)
            else:
                partial = jnp.zeros((trig_rows, channels), f32)
            rows_ref[h, pl.ds(l - low, trig_rows, stride=8), :] = partial
        for b in range(lon_count):
            got = []
            for r in range(2):
                first = (b * 2 + r) * slots
                got.append(
                    spread(
                        [rows_ref[h, (first + s) * 8 : (first + s + 1) * 8, :] for s in range(slots)],
                        per_dev,
                    )
                )
            for a in range(lat_count):
                send1[h, a, b] = jnp.concatenate([got[0][a], got[1][a]], 0).astype(bf16)

    def lat_exchange(h, send, recv, send_sem, recv_sem):
        finish = exchange(
            lat_peer,
            lat_count,
            my_lat,
            lambda other: send.at[h, other],
            lambda other: recv.at[h, other],
            lambda other: send_sem.at[h, other],
            lambda other: recv_sem.at[h, other],
        )
        recv[h, my_lat] = send[h, my_lat]
        return finish

    def lon_exchange(source, recv, send_sem, recv_sem):
        return exchange(
            lon_peer,
            lon_count,
            my_lon,
            source,
            lambda other: recv.at[other],
            lambda other: send_sem.at[other],
            lambda other: recv_sem.at[other],
        )

    halves = ((0, min(8, lat_rows)), (8, lat_rows))
    ordered = column_part(*halves[0], True)
    pl.semaphore_wait(barrier, lat_count + lon_count - 2)
    pack(0, *halves[0], ordered)
    finish1 = [lat_exchange(0, send1, recv1, lat_send1, lat_recv1)]
    finish_leg = lon_exchange(lambda other: legs.at[my_lon], legs, leg_send, leg_recv)
    ordered = column_part(*halves[1], False)
    pack(1, *halves[1], ordered)
    finish1.append(lat_exchange(1, send1, recv1, lat_send1, lat_recv1))

    diff_col = column_of(diff_ref[...], channels)
    diff_row = jnp.sum(jnp.where(chosen, diff_col, 0.0), 0, keepdims=True)
    diff_sorted = column_of(diff_row, channels)
    lane = iota((channels, wide), 1)
    mine = iota((channels, wide), 0) == (lane & (per_dev - 1)) + my_lat * per_dev
    diff_lane = jnp.sum(jnp.where(mine, diff_sorted, 0.0), 0, keepdims=True)
    degree = iota((top, wide), 0).astype(f32)
    damping = diff_lane * (degree * (degree + 1.0)) / float(top * top)
    slot_lane = (iota((waves, wide), 1) & (channels - 1)) // per_dev
    wave_lane = jnp.sum(
        jnp.where(iota((waves, wide), 0) == slot_lane + my_lon * slots, wave_col, 0.0), 0, keepdims=True
    )
    scale = 1.0 / (1.0 + damping)
    lane_slot = (iota((top, wide), 1) & (channels - 1)) // per_dev

    finish_leg()
    leg_back = [jnp.transpose(legs[b].astype(f32)).astype(bf16) for b in range(lon_count)]
    for finish in finish1:
        finish()
    for b in range(lon_count):
        chunks = []
        for h in range(2):
            for a in range(lat_count):
                chunk = recv1[h, a, b].astype(f32)
                chunks.append(jnp.concatenate([chunk[:8], chunk[8:]], 1))
        weighted = (jnp.concatenate(chunks, 0) * quad_col).astype(bf16)
        raw = jnp.dot(legs[b], weighted, preferred_element_type=f32)
        own = raw[:top]
        for s in range(1, slots):
            own = jnp.where(lane_slot == s, raw[s * top : (s + 1) * top], own)
        send2[b] = own.astype(bf16)
    finish2 = lon_exchange(lambda other: send2.at[other], recv2, lon_send2, lon_recv2)
    recv2[my_lon] = send2[my_lon]
    finish2()
    raw = recv2[0].astype(f32)
    for b in range(1, lon_count):
        raw = raw + recv2[b].astype(f32)
    spectral = jnp.where(degree >= wave_lane, raw * scale, 0.0)
    low = spectral.astype(bf16)
    low_ref[...] = low
    finish3 = lon_exchange(lambda other: low_ref, recv3, lon_send3, lon_recv3)
    recv3[my_lon] = low
    spec_ref[...] = spectral
    finish3()

    blocks = []
    for b in range(lon_count):
        coeffs = recv3[b].astype(f32)
        blocks.append(
            jnp.concatenate([jnp.where(lane_slot == s, coeffs, 0.0) for s in range(slots)], 0).astype(bf16)
        )
    finish4 = []
    band = 8 * lat_count
    for h in range(2):
        for b in range(lon_count):
            back = jnp.dot(leg_back[b][h * band : (h + 1) * band], blocks[b], preferred_element_type=f32)
            for a in range(lat_count):
                rows = back[a * 8 : (a + 1) * 8]
                send4[h, a, b] = jnp.concatenate([rows[:, :channels], rows[:, channels:]], 0).astype(bf16)
        finish4.append(lat_exchange(h, send4, recv4, lat_send4, lat_recv4))
    for h in range(2):
        finish4[h]()
        for b in range(lon_count):
            chunks = [recv4[h, a, b].astype(f32) for a in range(lat_count)]
            for r in range(2):
                first = (b * 2 + r) * slots
                got = spread([c[r * 8 : (r + 1) * 8] for c in chunks], per_dev)
                whole = jnp.concatenate(got, 0).astype(bf16)
                rows_ref[h, first * 8 : (first + slots) * 8, :] = jnp.dot(
                    whole, unorder, preferred_element_type=f32
                )
        for l in range(*halves[h]):
            coeffs = rows_ref[h, pl.ds(l - 8 * h, trig_rows, stride=8), :].astype(bf16)
            tendency = jnp.dot(trig_out, coeffs, preferred_element_type=f32).astype(bf16)
            here = slice(l * lon_cols, (l + 1) * lon_cols)
            out_ref[here, :] = (cols_ref[here, :].astype(f32) + tendency.astype(f32)).astype(bf16)


def fused(
    grid_state,
    weight_in,
    bias_in,
    weight_out,
    quad_weights,
    diffusion,
    legendre,
    chan_table,
    wave_table,
):
    lat_rows, lon_cols, channels = grid_state.shape
    lat_count = lax.axis_size("lat")
    lon_count = lax.axis_size("lon")
    slots, lat_total, top = legendre.shape
    waves = wave_table.shape[0]
    wide = 2 * channels
    bf16 = jnp.bfloat16
    vmem = pl.BlockSpec(memory_space=pltpu.VMEM)
    anywhere = pl.BlockSpec(memory_space=WEIGHTS)
    chunks = pltpu.VMEM((2, lat_count, lon_count, 16, channels), bf16)
    coeffs = pltpu.VMEM((lon_count, top, wide), bf16)
    lat_sems = pltpu.SemaphoreType.DMA((2, lat_count))
    lon_sems = pltpu.SemaphoreType.DMA((lon_count,))
    updated, spec = pl.pallas_call(
        functools.partial(fused_kernel, lat_count, lon_count, lat_rows, lon_cols, slots),
        out_shape=(
            jax.ShapeDtypeStruct((lat_rows * lon_cols, channels), bf16),
            jax.ShapeDtypeStruct((top, wide), jnp.float32),
        ),
        in_specs=[vmem, anywhere, vmem, anywhere] + [vmem] * 5,
        out_specs=(vmem, vmem),
        scratch_shapes=[
            pltpu.VMEM(weight_in.shape, bf16),
            pltpu.VMEM(weight_out.shape, bf16),
            pltpu.VMEM((lat_rows * lon_cols, channels), bf16),
            pltpu.VMEM((2, 2 * waves * 8, channels), jnp.float32),
            pltpu.VMEM((lon_count, slots * top, 16 * lat_count), bf16),
            chunks,
            chunks,
            coeffs,
            coeffs,
            pltpu.VMEM((top, wide), bf16),
            coeffs,
            chunks,
            chunks,
            pltpu.SemaphoreType.DMA((2, weight_in.shape[0])),
            lon_sems,
            lon_sems,
            lat_sems,
            lat_sems,
            lon_sems,
            lon_sems,
            lon_sems,
            lon_sems,
            lat_sems,
            lat_sems,
        ],
        compiler_params=pltpu.CompilerParams(
            collective_id=0, has_side_effects=True, vmem_limit_bytes=60 * 2**20
        ),
    )(
        grid_state.reshape(lat_rows * lon_cols, channels),
        weight_in,
        bias_in,
        weight_out,
        quad_weights[None, :],
        diffusion[None, :],
        legendre.swapaxes(1, 2).reshape(slots * top, lat_total),
        chan_table[None, :],
        wave_table[None, :],
    )
    spectral = spec.reshape(top, 2, slots, channels // lat_count).transpose(2, 3, 1, 0)
    return updated.reshape(lat_rows, lon_cols, channels), spectral


def by_size(*arrays):
    grid_state, legendre, wave_table = arrays[0], arrays[6], arrays[8]
    lat_rows, lon_cols, channels = grid_state.shape
    slots, _, top = legendre.shape
    fits = (
        channels == 128
        and slots == lax.axis_size("lat")
        and slots & (slots - 1) == 0
        and top & (top - 1) == 0
        and slots * lax.axis_size("lon") == wave_table.shape[0]
        and 8 < lat_rows <= 16
        and lon_cols % 16 == 0
    )
    return (fused if fits else local)(*arrays)


def solution(mesh):
    placed = (P("lat", "lon", None), P(), P(), P(), P(), P(), P("lon", None, None), P(), P())
    return jax.shard_map(
        by_size,
        mesh=mesh,
        in_specs=placed,
        out_specs=(P("lat", "lon", None), P("lon", "lat", None, None)),
        check_vma=False,
    )
```

```python
import functools
import math

import jax
import jax.numpy as jnp
from jax import lax
from jax.experimental import pallas as pl
from jax.experimental.pallas import tpu as pltpu
from jax.sharding import PartitionSpec as P

MESH = pl.DeviceIdType.MESH
WEIGHTS = pl.ANY
EARLY = 3
GELU_A = math.sqrt(2.0 / math.pi)
GELU_B = 0.044715 * GELU_A


def column_layers(column_rows, weight_in, bias_in, weight_out):
    hidden_state = column_rows.astype(jnp.float32)
    for layer_idx in range(weight_in.shape[0]):
        inv_rms = lax.rsqrt(jnp.mean(hidden_state * hidden_state, axis=-1, keepdims=True) + 1e-06)
        normed = (hidden_state * inv_rms).astype(jnp.bfloat16)
        pre_act = (
            jnp.dot(normed, weight_in[layer_idx], preferred_element_type=jnp.float32)
            + bias_in[layer_idx]
        )
        activation = jax.nn.gelu(pre_act, approximate=True).astype(jnp.bfloat16)
        hidden_state = hidden_state + jnp.dot(
            activation, weight_out[layer_idx], preferred_element_type=jnp.float32
        )
    return hidden_state.astype(jnp.bfloat16)


def trig_table(wave_ids, longitudes, lon_total):
    phase_angle = (wave_ids[:, None] * longitudes[None, :] % lon_total).astype(jnp.float32) * (
        2.0 * math.pi / lon_total
    )
    stacked = jnp.stack([jnp.cos(phase_angle), -jnp.sin(phase_angle)], axis=1) / math.sqrt(
        lon_total
    )
    return stacked.astype(jnp.bfloat16)


def pick_channels(rows, chosen):
    picked = jnp.einsum("ljc,ck->ljk", rows, chosen, preferred_element_type=jnp.float32)
    return picked.astype(jnp.bfloat16)


def local(
    grid_state,
    weight_in,
    bias_in,
    weight_out,
    quad_weights,
    diffusion,
    legendre,
    chan_table,
    wave_table,
):
    lat_rows, lon_cols, channels = grid_state.shape
    lat_count = lax.axis_size("lat")
    lon_count = lax.axis_size("lon")
    lon_total = lon_cols * lon_count
    per_dev = channels // lat_count
    owned_slots = legendre.shape[0]
    top_degree = legendre.shape[2]
    flat_rows = grid_state.reshape(lat_rows * lon_cols, channels)
    columns = column_layers(flat_rows, weight_in, bias_in, weight_out).reshape(
        lat_rows, lon_cols, channels
    )
    every = jnp.arange(channels, dtype=jnp.int32)
    chosen = (every[:, None] == chan_table[None, :]).astype(jnp.bfloat16)
    ordered = pick_channels(columns, chosen)
    levels = lax.all_to_all(ordered, "lat", split_axis=2, concat_axis=0, tiled=True)
    trig_all = trig_table(wave_table, jnp.arange(lon_total, dtype=jnp.int32), lon_total)
    lon_here = lax.axis_index("lon") * lon_cols + jnp.arange(lon_cols, dtype=jnp.int32)
    trig_rows = trig_table(wave_table, lon_here, lon_total)
    fourier = lax.psum_scatter(
        jnp.einsum("srj,ljk->skrl", trig_rows, levels, preferred_element_type=jnp.float32),
        "lon",
        scatter_dimension=0,
        tiled=True,
    )
    weighted = (fourier * quad_weights).astype(jnp.bfloat16)
    raw_spec = jnp.einsum("skrl,sln->skrn", weighted, legendre, preferred_element_type=jnp.float32)
    my_waves = lax.dynamic_slice_in_dim(
        wave_table, lax.axis_index("lon") * owned_slots, owned_slots, 0
    )
    degree = jnp.arange(top_degree, dtype=jnp.int32)
    triangle = (degree[None, :] >= my_waves[:, None]).astype(jnp.float32)
    my_chans = lax.dynamic_slice_in_dim(chan_table, lax.axis_index("lat") * per_dev, per_dev, 0)
    degree_f = degree.astype(jnp.float32)
    damping = (
        jnp.sum(jnp.where(my_chans[:, None] == every[None, :], diffusion[None, :], 0.0), 1)[:, None]
        * (degree_f * (degree_f + 1.0))[None, :]
        / float(top_degree * top_degree)
    )
    spectral = raw_spec * triangle[:, None, None, :] / (1.0 + damping)[None, :, None, :]
    back_fourier = jnp.einsum(
        "skrn,sln->skrl",
        spectral.astype(jnp.bfloat16),
        legendre,
        preferred_element_type=jnp.float32,
    ).astype(jnp.bfloat16)
    all_waves = lax.all_to_all(back_fourier, "lon", split_axis=3, concat_axis=0, tiled=True)
    band_tendency = jnp.einsum(
        "skrl,srj->ljk", all_waves, trig_all, preferred_element_type=jnp.float32
    ).astype(jnp.bfloat16)
    tendency = lax.all_to_all(
        lax.all_to_all(band_tendency, "lon", split_axis=1, concat_axis=0, tiled=True),
        "lat",
        split_axis=0,
        concat_axis=2,
        tiled=True,
    )
    tendency = pick_channels(tendency, chosen.T)
    updated = (columns.astype(jnp.float32) + tendency.astype(jnp.float32)).astype(jnp.bfloat16)
    return (updated, spectral)

def spread(blocks, width):
    blocks = list(blocks)
    group = lax.broadcasted_iota(jnp.int32, blocks[0].shape, 1) // width
    lanes = blocks[0].shape[1]
    step = 1
    while step < len(blocks):
        upper = (group & step) != 0
        for i in range(len(blocks)):
            if i & step == 0:
                low, high = blocks[i], blocks[i + step]
                blocks[i] = jnp.where(upper, pltpu.roll(high, step * width, 1), low)
                blocks[i + step] = jnp.where(
                    upper, high, pltpu.roll(low, lanes - step * width, 1)
                )
        step *= 2
    return blocks


def fused_kernel(
    lat_count,
    lon_count,
    lat_rows,
    lon_cols,
    slots,
    grid_ref,
    w_in_hbm,
    bias_ref,
    w_out_hbm,
    quad_ref,
    diff_ref,
    leg_ref,
    chan_ref,
    wave_ref,
    out_ref,
    spec_ref,
    w_in_ref,
    w_out_ref,
    cols_ref,
    rows_ref,
    legs,
    send1,
    recv1,
    send2,
    recv2,
    low_ref,
    recv3,
    send4,
    recv4,
    w_sem,
    leg_send,
    leg_recv,
    lat_send1,
    lat_recv1,
    lon_send2,
    lon_recv2,
    lon_send3,
    lon_recv3,
    lat_send4,
    lat_recv4,
):
    f32, bf16, i32 = jnp.float32, jnp.bfloat16, jnp.int32
    iota = lambda shape, dim: lax.broadcasted_iota(i32, shape, dim)
    channels = grid_ref.shape[1]
    layers = w_in_ref.shape[0]
    spect, lat_total = leg_ref.shape
    top = spect // slots
    waves = wave_ref.shape[1]
    per_dev = channels // lat_count
    wide = 2 * channels
    trig_rows = 2 * waves
    lon_total = lon_cols * lon_count
    my_lat, my_lon = lax.axis_index("lat"), lax.axis_index("lon")

    loads = []
    for layer in range(layers):
        into = pltpu.make_async_copy(w_in_hbm.at[layer], w_in_ref.at[layer], w_sem.at[0, layer])
        out_of = pltpu.make_async_copy(w_out_hbm.at[layer], w_out_ref.at[layer], w_sem.at[1, layer])
        into.start()
        out_of.start()
        loads.append((into, out_of))

    barrier = pltpu.get_barrier_semaphore()

    def lat_peer(i):
        other = lax.rem(my_lat + i, lat_count)
        return other, {"lat": other, "lon": my_lon}

    def lon_peer(i):
        other = lax.rem(my_lon + i, lon_count)
        return other, {"lat": my_lat, "lon": other}

    for i in range(1, lat_count):
        pl.semaphore_signal(barrier, inc=1, device_id=lat_peer(i)[1], device_id_type=MESH)
    for i in range(1, lon_count):
        pl.semaphore_signal(barrier, inc=1, device_id=lon_peer(i)[1], device_id_type=MESH)

    sent = []

    def exchange(peer_of, count, mine, source, target, send_sem, recv_sem):
        waits = []
        for i in range(1, count):
            other, place = peer_of(i)
            pltpu.make_async_remote_copy(
                src_ref=source(other),
                dst_ref=target(mine),
                send_sem=send_sem(other),
                recv_sem=recv_sem(mine),
                device_id=place,
                device_id_type=MESH,
            ).start()
            waits.append(
                pltpu.make_async_remote_copy(
                    src_ref=source(other),
                    dst_ref=target(other),
                    send_sem=send_sem(other),
                    recv_sem=recv_sem(other),
                    device_id=place,
                    device_id_type=MESH,
                )
            )

        sent.extend(waits)

        def finish():
            for w in waits:
                w.wait_recv()

        return finish

    def column_of(row, size):
        eye = iota((size, size), 0) == iota((size, size), 1)
        return jnp.sum(jnp.where(eye, row, jnp.zeros_like(row)), 1, keepdims=True)

    chan_row = chan_ref[...]
    chosen = iota((channels, channels), 0) == chan_row
    order = jnp.where(chosen, 1.0, 0.0).astype(bf16)
    unorder = jnp.where(iota((channels, channels), 1) == column_of(chan_row, channels), 1.0, 0.0)
    unorder = unorder.astype(bf16)

    wave_f = wave_ref[...].astype(f32)
    wave_col = column_of(wave_f, waves)

    def slot_of(row):
        inner = row & (2 * slots - 1)
        return (row // (2 * slots)) * slots + (inner & (slots - 1)), inner // slots

    def trig(wave, part, place):
        angle = wave * place
        angle = angle + part * (lon_total / 4.0)
        angle = angle - lon_total * jnp.floor((angle + 0.5) * (1.0 / lon_total))
        return jnp.cos(angle * (2.0 * math.pi / lon_total)) * (1.0 / math.sqrt(lon_total))

    slot_a, part_a = slot_of(iota((trig_rows, 1), 0))
    wave_a = jnp.sum(jnp.where(iota((trig_rows, waves), 1) == slot_a, wave_f, 0.0), 1, keepdims=True)
    lon_a = (iota((trig_rows, lon_cols), 1) + my_lon * lon_cols).astype(f32)
    trig_in = trig(wave_a, part_a.astype(f32), lon_a).astype(bf16)
    slot_b, part_b = slot_of(iota((1, trig_rows), 1))
    wave_b = jnp.sum(jnp.where(iota((waves, trig_rows), 0) == slot_b, wave_col, 0.0), 0, keepdims=True)
    lon_b = (iota((lon_cols, trig_rows), 0) + my_lon * lon_cols).astype(f32)
    trig_out = trig(wave_b, part_b.astype(f32), lon_b).astype(bf16)

    lat_pad = 16 * lat_count

    def lat_of(place):
        row = (place // (8 * lat_count)) * 8 + (place & 7)
        device = (place // 8) & (lat_count - 1)
        return jnp.where(row < lat_rows, device * lat_rows + row, -1)

    by_row = lat_of(iota((lat_pad, lat_total), 0)) == iota((lat_pad, lat_total), 1)
    quad_col = jnp.sum(jnp.where(by_row, quad_ref[...], 0.0), 1, keepdims=True)
    lat_col = iota((lat_total, lat_pad), 0)
    by_col = jnp.where(lat_of(iota((lat_total, lat_pad), 1)) == lat_col, 1.0, 0.0).astype(bf16)
    legs[my_lon] = jnp.dot(leg_ref[...], by_col, preferred_element_type=f32).astype(bf16)

    finish_leg = []

    def send_legendre():
        pl.semaphore_wait(barrier, lat_count + lon_count - 2)
        finish_leg.append(lon_exchange(lambda other: legs.at[my_lon], legs, leg_send, leg_recv))

    def column_part(low, high, first):
        part = slice(low * lon_cols, high * lon_cols)
        x = grid_ref[part, :].astype(f32)
        for layer in range(layers):
            inv = lax.rsqrt(jnp.mean(x * x, axis=-1, keepdims=True) + 1e-06)
            normed = (x * inv).astype(bf16)
            if first:
                loads[layer][0].wait()
            pre = jnp.dot(normed, w_in_ref[layer], preferred_element_type=f32)
            pre = pre + bias_ref[pl.ds(layer, 1), :]
            inner = pre * (GELU_A + GELU_B * (pre * pre))
            half = 0.5 * pre
            act = (half + half * jnp.tanh(inner)).astype(bf16)
            if first:
                loads[layer][1].wait()
            x = x + jnp.dot(act, w_out_ref[layer], preferred_element_type=f32)
            if first and layer == EARLY:
                send_legendre()
        cols = x.astype(bf16)
        cols_ref[part, :] = cols
        return jnp.dot(cols, order, preferred_element_type=f32).astype(bf16)

    def pack(h, low, high, ordered):
        for l in range(low, low + 8):
            if l < high:
                q = (l - low) * lon_cols
                partial = jnp.dot(trig_in, ordered[q : q + lon_cols], preferred_element_type=f32)
            else:
                partial = jnp.zeros((trig_rows, channels), f32)
            rows_ref[h, pl.ds(l - low, trig_rows, stride=8), :] = partial
        for b in range(lon_count):
            got = []
            for r in range(2):
                first = (b * 2 + r) * slots
                got.append(
                    spread(
                        [rows_ref[h, (first + s) * 8 : (first + s + 1) * 8, :] for s in range(slots)],
                        per_dev,
                    )
                )
            for a in range(lat_count):
                send1[h, a, b] = jnp.concatenate([got[0][a], got[1][a]], 0).astype(bf16)

    def lat_exchange(h, send, recv, send_sem, recv_sem):
        finish = exchange(
            lat_peer,
            lat_count,
            my_lat,
            lambda other: send.at[h, other],
            lambda other: recv.at[h, other],
            lambda other: send_sem.at[h, other],
            lambda other: recv_sem.at[h, other],
        )
        recv[h, my_lat] = send[h, my_lat]
        return finish

    def lon_exchange(source, recv, send_sem, recv_sem):
        return exchange(
            lon_peer,
            lon_count,
            my_lon,
            source,
            lambda other: recv.at[other],
            lambda other: send_sem.at[other],
            lambda other: recv_sem.at[other],
        )

    halves = ((0, min(8, lat_rows)), (8, lat_rows))
    ordered = column_part(*halves[0], True)
    pack(0, *halves[0], ordered)
    finish1 = [lat_exchange(0, send1, recv1, lat_send1, lat_recv1)]
    ordered = column_part(*halves[1], False)
    pack(1, *halves[1], ordered)
    finish1.append(lat_exchange(1, send1, recv1, lat_send1, lat_recv1))

    diff_col = column_of(diff_ref[...], channels)
    diff_row = jnp.sum(jnp.where(chosen, diff_col, 0.0), 0, keepdims=True)
    diff_sorted = column_of(diff_row, channels)
    lane = iota((channels, wide), 1)
    mine = iota((channels, wide), 0) == (lane & (per_dev - 1)) + my_lat * per_dev
    diff_lane = jnp.sum(jnp.where(mine, diff_sorted, 0.0), 0, keepdims=True)
    degree = iota((top, wide), 0).astype(f32)
    damping = diff_lane * (degree * (degree + 1.0)) / float(top * top)
    slot_lane = (iota((waves, wide), 1) & (channels - 1)) // per_dev
    wave_lane = jnp.sum(
        jnp.where(iota((waves, wide), 0) == slot_lane + my_lon * slots, wave_col, 0.0), 0, keepdims=True
    )
    scale = 1.0 / (1.0 + damping)
    lane_slot = (iota((top, wide), 1) & (channels - 1)) // per_dev

    finish_leg[0]()
    leg_back = [jnp.transpose(legs[b].astype(f32)).astype(bf16) for b in range(lon_count)]
    for finish in finish1:
        finish()
    for b in range(lon_count):
        chunks = []
        for h in range(2):
            for a in range(lat_count):
                chunk = recv1[h, a, b].astype(f32)
                chunks.append(jnp.concatenate([chunk[:8], chunk[8:]], 1))
        weighted = (jnp.concatenate(chunks, 0) * quad_col).astype(bf16)
        raw = jnp.dot(legs[b], weighted, preferred_element_type=f32)
        own = raw[:top]
        for s in range(1, slots):
            own = jnp.where(lane_slot == s, raw[s * top : (s + 1) * top], own)
        send2[b] = own.astype(bf16)
    finish2 = lon_exchange(lambda other: send2.at[other], recv2, lon_send2, lon_recv2)
    recv2[my_lon] = send2[my_lon]
    finish2()
    raw = recv2[0].astype(f32)
    for b in range(1, lon_count):
        raw = raw + recv2[b].astype(f32)
    spectral = jnp.where(degree >= wave_lane, raw * scale, 0.0)
    low = spectral.astype(bf16)
    low_ref[...] = low
    finish3 = lon_exchange(lambda other: low_ref, recv3, lon_send3, lon_recv3)
    recv3[my_lon] = low
    by_channel = jnp.transpose(spectral)
    for r in range(2):
        spec_ref[:, r, :] = by_channel[r * channels : (r + 1) * channels]
    finish3()

    blocks = []
    for b in range(lon_count):
        coeffs = recv3[b].astype(f32)
        blocks.append(
            jnp.concatenate([jnp.where(lane_slot == s, coeffs, 0.0) for s in range(slots)], 0).astype(bf16)
        )
    finish4 = []
    band = 8 * lat_count
    for h in range(2):
        for b in range(lon_count):
            back = jnp.dot(leg_back[b][h * band : (h + 1) * band], blocks[b], preferred_element_type=f32)
            for a in range(lat_count):
                rows = back[a * 8 : (a + 1) * 8]
                send4[h, a, b] = jnp.concatenate([rows[:, :channels], rows[:, channels:]], 0).astype(bf16)
        finish4.append(lat_exchange(h, send4, recv4, lat_send4, lat_recv4))
    for h in range(2):
        finish4[h]()
        for b in range(lon_count):
            chunks = [recv4[h, a, b].astype(f32) for a in range(lat_count)]
            for r in range(2):
                first = (b * 2 + r) * slots
                got = spread([c[r * 8 : (r + 1) * 8] for c in chunks], per_dev)
                whole = jnp.concatenate(got, 0).astype(bf16)
                rows_ref[h, first * 8 : (first + slots) * 8, :] = jnp.dot(
                    whole, unorder, preferred_element_type=f32
                )
        for l in range(*halves[h]):
            coeffs = rows_ref[h, pl.ds(l - 8 * h, trig_rows, stride=8), :].astype(bf16)
            tendency = jnp.dot(trig_out, coeffs, preferred_element_type=f32).astype(bf16)
            here = slice(l * lon_cols, (l + 1) * lon_cols)
            out_ref[here, :] = (cols_ref[here, :].astype(f32) + tendency.astype(f32)).astype(bf16)
    for copy in sent:
        copy.wait_send()


def fused(
    grid_state,
    weight_in,
    bias_in,
    weight_out,
    quad_weights,
    diffusion,
    legendre,
    chan_table,
    wave_table,
):
    lat_rows, lon_cols, channels = grid_state.shape
    lat_count = lax.axis_size("lat")
    lon_count = lax.axis_size("lon")
    slots, lat_total, top = legendre.shape
    waves = wave_table.shape[0]
    wide = 2 * channels
    bf16 = jnp.bfloat16
    vmem = pl.BlockSpec(memory_space=pltpu.VMEM)
    anywhere = pl.BlockSpec(memory_space=WEIGHTS)
    chunks = pltpu.VMEM((2, lat_count, lon_count, 16, channels), bf16)
    coeffs = pltpu.VMEM((lon_count, top, wide), bf16)
    lat_sems = pltpu.SemaphoreType.DMA((2, lat_count))
    lon_sems = pltpu.SemaphoreType.DMA((lon_count,))
    updated, spec = pl.pallas_call(
        functools.partial(fused_kernel, lat_count, lon_count, lat_rows, lon_cols, slots),
        out_shape=(
            jax.ShapeDtypeStruct((lat_rows * lon_cols, channels), bf16),
            jax.ShapeDtypeStruct((channels, 2, top), jnp.float32),
        ),
        in_specs=[vmem, anywhere, vmem, anywhere] + [vmem] * 5,
        out_specs=(vmem, vmem),
        scratch_shapes=[
            pltpu.VMEM(weight_in.shape, bf16),
            pltpu.VMEM(weight_out.shape, bf16),
            pltpu.VMEM((lat_rows * lon_cols, channels), bf16),
            pltpu.VMEM((2, 2 * waves * 8, channels), jnp.float32),
            pltpu.VMEM((lon_count, slots * top, 16 * lat_count), bf16),
            chunks,
            chunks,
            coeffs,
            coeffs,
            pltpu.VMEM((top, wide), bf16),
            coeffs,
            chunks,
            chunks,
            pltpu.SemaphoreType.DMA((2, weight_in.shape[0])),
            lon_sems,
            lon_sems,
            lat_sems,
            lat_sems,
            lon_sems,
            lon_sems,
            lon_sems,
            lon_sems,
            lat_sems,
            lat_sems,
        ],
        compiler_params=pltpu.CompilerParams(
            collective_id=0, has_side_effects=True, vmem_limit_bytes=60 * 2**20
        ),
    )(
        grid_state.reshape(lat_rows * lon_cols, channels),
        weight_in,
        bias_in,
        weight_out,
        quad_weights[None, :],
        diffusion[None, :],
        legendre.swapaxes(1, 2).reshape(slots * top, lat_total),
        chan_table[None, :],
        wave_table[None, :],
    )
    spectral = spec.reshape(slots, channels // lat_count, 2, top)
    return updated.reshape(lat_rows, lon_cols, channels), spectral


def by_size(*arrays):
    grid_state, legendre, wave_table = arrays[0], arrays[6], arrays[8]
    lat_rows, lon_cols, channels = grid_state.shape
    slots, _, top = legendre.shape
    fits = (
        channels == 128
        and slots == lax.axis_size("lat")
        and slots & (slots - 1) == 0
        and top & (top - 1) == 0
        and slots * lax.axis_size("lon") == wave_table.shape[0]
        and 8 < lat_rows <= 16
        and lon_cols % 16 == 0
    )
    return (fused if fits else local)(*arrays)


def solution(mesh):
    placed = (P("lat", "lon", None), P(), P(), P(), P(), P(), P("lon", None, None), P(), P())
    return jax.shard_map(
        by_size,
        mesh=mesh,
        in_specs=placed,
        out_specs=(P("lat", "lon", None), P("lon", "lat", None, None)),
        check_vma=False,
    )
```
